256 devices in a mesh: seq: 64 (over y, z_hi, x), tp: 4 (over z_lo, core).
Axes of the slice: x: 4, y: 4, z: 8 (z_hi: 4, z_lo: 2; z = z_hi * 2 + z_lo), core: 2. Of those that a mesh axis runs over, the one named last changes fastest.
Arguments:
- sequence_in: bfloat16 [16384, 4096], P('seq'), may hold values from -6 to 6
- value_proj: bfloat16 [4096, 4096], P('seq', 'tp'), may hold values from -0.09375 to 0.09375
- gate_proj: bfloat16 [4096, 4096], P('seq', 'tp'), may hold values from -0.09375 to 0.09375
- filter_response: bfloat16 [2, 256, 64, 4096], P(None, None, 'seq', 'tp'), may hold values from -6 to 6
- skip_weight: float32 [4096], P('tp'), may hold values from -1 to 1
- output_proj: bfloat16 [4096, 4096], P('tp'), may hold values from -0.09375 to 0.09375
Outputs:
- layer_out: bfloat16 [16384, 4096], P('seq', 'tp')
The draws below stay inside these ranges and needn't reach their ends.
All inputs are finite; a program needn't handle non-finite values.
Results may differ from the reference program's by a relative error of at most 0.024.
Values may be sent and summed in bfloat16 or wider, within the bound.
No kernel may reach another device: no remote copies, remote signals or barrier semaphores. Data moves between devices by JAX's collectives and lax.ppermute only.
A program may use at most 128 MiB of HBM per device.

```python
import jax
import jax.numpy as jnp
from jax import lax

D = 4096
L_DEV = 256
TOKENS = 16384
GROUPS = 4
N_SEQ = 64


def block_scale(key, shape, split, smallest, high):
    gain, own = 1.0, jax.random.fold_in(key, 6)
    for axis_at, shards_of in split:
        draws = jnp.exp(jax.random.uniform(jax.random.fold_in(own, axis_at), (shards_of,), jnp.float32, smallest / len(split), high / len(split)))
        gain = gain * jnp.repeat(draws, shape[axis_at] // shards_of).reshape([-1 if axis == axis_at else 1 for axis in range(len(shape))])
    return gain


def centred(key, extent, spread, bound, pieces=(), held_as=jnp.bfloat16):
    gain = block_scale(key, extent, pieces, -0.22, 0.18) if pieces else 1.0
    array = jax.random.normal(key, extent, jnp.float32) * spread * gain
    return jnp.minimum(jnp.maximum(array, -bound), bound).astype(held_as)


def setup_inputs(seed: int = 0) -> dict:
    key_list = jax.random.split(jax.random.key(seed), 7)
    sequence_in = centred(key_list[0], (TOKENS, D), 1.0, 6.0, ((0, 64),))
    value_proj = centred(key_list[1], (D, D), D ** -0.5, 0.09375, ((0, 64), (1, 4)))
    gate_proj = centred(key_list[2], (D, D), D ** -0.5, 0.09375, ((0, 64), (1, 4)))
    filter_response = centred(key_list[3], (2, L_DEV, N_SEQ, D), 1.0, 6.0, ((2, 64), (3, 4)))
    skip_weight = jnp.clip(jax.random.uniform(key_list[4], (D,), jnp.float32, -1.0, 1.0) * block_scale(key_list[4], (D,), ((0, 4),), -0.4, 0.0), -1.0, 1.0)
    output_proj = centred(key_list[5], (D, D), D ** -0.5, 0.09375, ((0, 4),))
    return {"sequence_in": sequence_in, "value_proj": value_proj, "gate_proj": gate_proj, "filter_response": filter_response, "skip_weight": skip_weight, "output_proj": output_proj}


def filter_block(pair):
    signal_block, response_block = pair
    transformed = jnp.fft.fft(signal_block, axis=0)
    return jnp.real(jnp.fft.ifft(transformed * response_block, axis=0))


def reference(sequence_in, value_proj, gate_proj, filter_response, skip_weight, output_proj):
    value_part = jnp.dot(sequence_in, value_proj, preferred_element_type=jnp.float32).astype(jnp.bfloat16)
    gate_part = jnp.dot(sequence_in, gate_proj, preferred_element_type=jnp.float32).astype(jnp.bfloat16)
    block_width = min(D, 512)
    block_count = D // block_width
    signal = value_part.astype(jnp.float32).reshape(TOKENS, block_count, block_width).transpose(1, 0, 2)
    spectra = filter_response.astype(jnp.float32).reshape(2, TOKENS, block_count, block_width).transpose(0, 2, 1, 3)
    response = lax.complex(spectra[0], spectra[1])
    filtered = lax.map(filter_block, (signal, response))
    conv_part = filtered.transpose(1, 0, 2).reshape(TOKENS, D).astype(jnp.bfloat16)
    mixed = (gate_part.astype(jnp.float32) * (conv_part.astype(jnp.float32) + skip_weight * value_part.astype(jnp.float32))).astype(jnp.bfloat16)
    group_width = D // GROUPS
    summed = jnp.zeros((TOKENS, D), jnp.float32)
    for group_index in range(GROUPS):
        lower = group_index * group_width
        partial_sum = jnp.dot(mixed[:, lower:lower + group_width], output_proj[lower:lower + group_width], preferred_element_type=jnp.float32)
        rounded = lax.optimization_barrier(partial_sum.astype(jnp.bfloat16))
        summed = summed + rounded.astype(jnp.float32)
    return summed.astype(jnp.bfloat16)
```

```python
import math

import jax
import jax.numpy as jnp
import numpy as np
from jax import lax
from jax.sharding import Mesh
from jax.sharding import PartitionSpec as P

F32 = jnp.float32
BF16 = jnp.bfloat16
SEQ = ("y", "zh", "x")
SLABS = ("y", "zh")
UP = [(i, (i + 1) % 4) for i in range(4)]
DOWN = [(i, (i + 3) % 4) for i in range(4)]
SWAP = [(0, 1), (1, 0)]


def shift(count):
    return [(i, (i + count) % 4) for i in range(4)]


def ring_gather(block, axis):
    half = block.shape[0] // 2
    prev = lax.ppermute(block, axis, UP)
    nxt = lax.ppermute(block, axis, DOWN)
    far = jnp.concatenate(
        [lax.ppermute(prev[:half], axis, UP), lax.ppermute(nxt[half:], axis, DOWN)]
    )
    return [block, nxt, far, prev]


def place(blocks, axis):
    rows = blocks[0].shape[0]
    own = lax.axis_index(axis)
    whole = jnp.zeros((4 * rows, blocks[0].shape[1]), blocks[0].dtype)
    for step, block in enumerate(blocks):
        whole = lax.dynamic_update_slice(whole, block, ((own + step) % 4 * rows, 0))
    return whole


def gather_weights(shard):
    rows, cols = shard.shape
    split = shard.reshape(rows, 4, cols // 4).transpose(1, 0, 2)
    mine = lax.all_to_all(split, "x", 0, 0).reshape(4 * rows, cols // 4)
    mine = place(ring_gather(mine, "zh"), "zh")
    return place(ring_gather(mine, "y"), "y")


def inner_tables(count):
    idx = np.arange(count)
    angle = (idx[:, None] * idx[None, :] % count) * (2.0 * math.pi / count)
    cos, sin = np.cos(angle), np.sin(angle)
    ahead = np.block([[cos, -sin], [sin, cos]])
    back = np.block([[cos, sin], [-sin, cos]])
    return jnp.asarray(ahead, BF16), jnp.asarray(back, BF16)


def mm(left, right):
    return jnp.dot(left, right, preferred_element_type=F32)


def body(sequence_in, value_proj, gate_proj, filter_response, skip_weight, output_proj):
    rows = sequence_in.shape[0]
    half = rows // 2
    my_x = lax.axis_index("x")
    my_c = lax.axis_index("c")
    full = rows * 64

    resp = filter_response[:, :, 0, :].reshape(2, rows, 4, 16, 16)
    resp = resp.transpose(3, 2, 4, 0, 1).reshape(64, 16, 2 * rows)
    resp = lax.all_to_all(resp, SEQ, 0, 0, tiled=True).astype(F32)

    own = lax.dynamic_slice(sequence_in, (my_c * half, 0), (half, sequence_in.shape[1]))
    other = lax.dynamic_slice(sequence_in, ((1 - my_c) * half, 0), (half, sequence_in.shape[1]))
    mine = ring_gather(own, "x")
    rest = [other] + [lax.ppermute(b, "c", SWAP) for b in mine[1:]]
    act = jnp.concatenate([p for pair in zip(mine, rest) for p in pair])

    def project(weights):
        prod = mm(act, weights).astype(BF16)
        return prod.reshape(4, rows, 16, 16).transpose(2, 0, 3, 1)

    value = project(gather_weights(value_proj))
    gate = project(gather_weights(gate_proj))

    slabs = lax.all_to_all(value, SLABS, 0, 0, tiled=True).reshape(64, 16, rows)

    s_idx = lax.iota(jnp.int32, 64)
    s_idx = s_idx // 4 * 4 + (s_idx % 4 + my_x) % 4
    k_idx = lax.iota(jnp.int32, 64)
    slab_angle = (k_idx[:, None] * s_idx[None, :] % 64).astype(F32) * (2.0 * math.pi / 64)
    slab_cos, slab_sin = jnp.cos(slab_angle), jnp.sin(slab_angle)
    first = jnp.concatenate([slab_cos, -slab_sin]).astype(BF16)
    last = (jnp.concatenate([slab_cos, -slab_sin]) / full).astype(BF16)
    r_idx = (lax.iota(jnp.int32, rows) + my_c * half) % rows
    twist = (k_idx[:, None] * r_idx[None, :]).astype(F32) * (2.0 * math.pi / full)
    t_cos, t_sin = jnp.cos(twist)[:, None, :], jnp.sin(twist)[:, None, :]
    ahead, back = inner_tables(rows)

    sect = jnp.einsum("ks,scr->kcr", first, slabs, preferred_element_type=F32)
    re, im = sect[:64], sect[64:]
    turned = jnp.concatenate([re * t_cos + im * t_sin, im * t_cos - re * t_sin], axis=2)
    spec = mm(turned.astype(BF16), ahead)
    re, im = spec[..., :rows], spec[..., rows:]
    h_re, h_im = resp[..., :rows], resp[..., rows:]
    prod = jnp.concatenate([re * h_re - im * h_im, re * h_im + im * h_re], axis=2)
    inv = mm(prod.astype(BF16), back)
    re, im = inv[..., :rows], inv[..., rows:]
    reverted = jnp.concatenate([re * t_cos - im * t_sin, re * t_sin + im * t_cos], axis=0)
    conv = jnp.einsum("ks,kcr->scr", last, reverted.astype(BF16), preferred_element_type=F32)
    conv = conv.astype(BF16).reshape(16, 4, 16, rows)
    conv = lax.all_to_all(conv, SLABS, 0, 0, tiled=True)

    skip = lax.dynamic_slice(skip_weight, (my_x * 256,), (256,)).reshape(16, 1, 16, 1)
    mixed = (
        gate.astype(F32) * (conv.astype(F32) + skip * value.astype(F32))
    ).astype(BF16)

    home = jnp.zeros((1024, rows), BF16)
    for step in range(4):
        piece = mixed[:, step].reshape(256, rows)
        if step:
            piece = lax.ppermute(piece, "x", shift(step))
        home = lax.dynamic_update_slice(home, piece, ((my_x - step) % 4 * 256, 0))
    home = jnp.where(my_c == 0, home, jnp.roll(home, half, axis=1))

    part = lax.dot_general(
        home, output_proj, (((0,), (0,)), ((), ())), preferred_element_type=F32
    ).astype(BF16)
    part = part.reshape(rows, 2, 2, 1024)
    keep = jnp.where(my_c == 0, part[:, :, 0], part[:, :, 1])
    give = jnp.where(my_c == 0, part[:, :, 1], part[:, :, 0])
    pair = keep.astype(F32) + lax.ppermute(give, "c", SWAP).astype(F32)
    my_z = lax.axis_index("zl")
    keep = jnp.where(my_z == 0, pair[:, 0], pair[:, 1])
    give = jnp.where(my_z == 0, pair[:, 1], pair[:, 0]).astype(BF16)
    return (keep + lax.ppermute(give, "zl", SWAP).astype(F32)).astype(BF16)


def solution(mesh):
    fine = Mesh(mesh.devices.reshape(4, 4, 4, 2, 2), ("y", "zh", "x", "zl", "c"))
    tp = ("zl", "c")
    placed = (
        P(SEQ, None),
        P(SEQ, tp),
        P(SEQ, tp),
        P(None, None, SEQ, tp),
        P(tp),
        P(tp, None),
    )
    return jax.shard_map(
        body, mesh=fine, in_specs=placed, out_specs=P(SEQ, tp), check_vma=False
    )
```

```python
import math

import jax
import jax.numpy as jnp
import numpy as np
from jax import lax
from jax.experimental import pallas as pl
from jax.experimental.pallas import tpu as pltpu
from jax.sharding import Mesh
from jax.sharding import PartitionSpec as P

F32 = jnp.float32
BF16 = jnp.bfloat16
SEQ = ("y", "zh", "x")
SLABS = ("y", "zh")
SWAP = [(0, 1), (1, 0)]


def shift(count):
    return [(i, (i + count) % 4) for i in range(4)]


def tie(*arrays):
    return lax.optimization_barrier(arrays)


def in_hbm(arrays):
    return [pltpu.with_memory_space_constraint(a, pltpu.HBM) for a in arrays]


def spread(first, second):
    rows, cols = first.shape
    both = jnp.stack([first, second]).reshape(2, rows, 4, cols // 4).transpose(2, 0, 1, 3)
    both = jnp.broadcast_to(both[None], (4, 4, 2, rows, cols // 4))
    both = lax.all_to_all(
        both.reshape(16, 2, rows, cols // 4), ("zh", "x"), 0, 0, tiled=True
    )
    return tuple(both[:, at].reshape(16 * rows, cols // 4) for at in range(2))


def project_kernel(own_ref, act_ref, *refs):
    w_refs, (out, a_buf, w_buf, sems) = refs[:-4], refs[-4:]
    rows, block = a_buf.shape[1], w_buf.shape[0] // len(w_refs)
    copies = []
    for step, source in enumerate(w_refs):
        row = pl.multiple_of(lax.rem(own_ref[0] + 4 - step, 4) * block, 16)
        copies.append((source, w_buf.at[pl.ds(row, block)]))
    for part in range(4):
        copies.append((act_ref.at[pl.ds(part * rows, rows)], a_buf.at[part]))
    copies = [
        pltpu.make_async_copy(src, dst, sems.at[at]) for at, (src, dst) in enumerate(copies)
    ]
    for copy in copies:
        copy.start()
    for copy in copies[: len(w_refs)]:
        copy.wait()
    for part in range(4):
        copies[len(w_refs) + part].wait()
        prod = jnp.dot(a_buf[part], w_buf[...], preferred_element_type=F32)
        out[:, part] = prod.T.astype(BF16).reshape(16, 16, rows)


def project(own, act, weights):
    rows, depth = act.shape[0] // 4, act.shape[1]
    cols = weights[0].shape[1]
    count = len(weights) + 4
    return pl.pallas_call(
        project_kernel,
        out_shape=jax.ShapeDtypeStruct((16, 4, cols // 16, rows), BF16),
        in_specs=[pl.BlockSpec(memory_space=pltpu.SMEM)]
        + [pl.BlockSpec(memory_space=pltpu.HBM)] * (len(weights) + 1),
        out_specs=pl.BlockSpec(memory_space=pltpu.VMEM),
        scratch_shapes=[
            pltpu.VMEM((4, rows, depth), BF16),
            pltpu.VMEM((depth, cols), BF16),
            pltpu.SemaphoreType.DMA((count,)),
        ],
        compiler_params=pltpu.CompilerParams(vmem_limit_bytes=40 * 1024 * 1024),
    )(own.reshape(1), *in_hbm([act, *weights]))


def give_kernel(at_ref, *refs):
    pieces, (weight_ref, home_ref, give_ref, w_buf, sems) = refs[:4], refs[4:]
    own_x, own_c = at_ref[1], at_ref[2]
    width = w_buf.shape[2]
    copies = []
    for block in range(2):
        col = pl.multiple_of((2 * block + 1 - own_c) * width, 128)
        copies.append(
            pltpu.make_async_copy(
                weight_ref.at[:, pl.ds(col, width)], w_buf.at[block], sems.at[block]
            )
        )
        copies[-1].start()
    for step in range(4):
        src = lax.rem(own_x + 4 - step, 4)
        col = pl.multiple_of(src * 256, 128)
        home_ref[:, pl.ds(col, 256)] = pieces[step][...].astype(F32).T.astype(BF16)
    for block in range(2):
        copies[block].wait()
        give_ref[block] = jnp.dot(
            home_ref[...], w_buf[block], preferred_element_type=F32
        ).astype(BF16)


def home_and_give(at, pieces, weight):
    rows = pieces[0].shape[1]
    inside = pl.BlockSpec(memory_space=pltpu.VMEM)
    return pl.pallas_call(
        give_kernel,
        out_shape=(
            jax.ShapeDtypeStruct((rows, 1024), BF16),
            jax.ShapeDtypeStruct((2, rows, 1024), BF16),
        ),
        in_specs=[pl.BlockSpec(memory_space=pltpu.SMEM)]
        + [inside] * 4
        + [pl.BlockSpec(memory_space=pltpu.HBM)],
        out_specs=(inside, inside),
        scratch_shapes=[pltpu.VMEM((2, 1024, 1024), BF16), pltpu.SemaphoreType.DMA((2,))],
        compiler_params=pltpu.CompilerParams(vmem_limit_bytes=32 * 1024 * 1024),
    )(at, *pieces, *in_hbm([weight]))


def keep_kernel(at_ref, home_ref, weight_ref, away_ref, mine_ref, w_buf, sems):
    own_z, own_c = at_ref[3], at_ref[2]
    width = w_buf.shape[2]
    copies = []
    for block in range(2):
        chip = lax.rem(own_z + 1 + block, 2)
        col = pl.multiple_of((2 * chip + own_c) * width, 128)
        copies.append(
            pltpu.make_async_copy(
                weight_ref.at[:, pl.ds(col, width)], w_buf.at[block], sems.at[block]
            )
        )
        copies[-1].start()
    for block, out_ref in enumerate((away_ref, mine_ref)):
        copies[block].wait()
        out_ref[...] = jnp.dot(home_ref[...], w_buf[block], preferred_element_type=F32)


def keep(at, home, weight):
    rows = home.shape[0]
    inside = pl.BlockSpec(memory_space=pltpu.VMEM)
    one = jax.ShapeDtypeStruct((rows, 1024), F32)
    return pl.pallas_call(
        keep_kernel,
        out_shape=(one, one),
        in_specs=[
            pl.BlockSpec(memory_space=pltpu.SMEM),
            inside,
            pl.BlockSpec(memory_space=pltpu.HBM),
        ],
        out_specs=(inside, inside),
        scratch_shapes=[pltpu.VMEM((2, 1024, 1024), BF16), pltpu.SemaphoreType.DMA((2,))],
        compiler_params=pltpu.CompilerParams(vmem_limit_bytes=32 * 1024 * 1024),
    )(at, home, *in_hbm([weight]))


def inner_tables(count):
    idx = np.arange(count)
    angle = (idx[:, None] * idx[None, :] % count) * (2.0 * math.pi / count)
    cos, sin = np.cos(angle), np.sin(angle)
    ahead = np.block([[cos, -sin], [sin, cos]])
    back = np.block([[cos, sin], [-sin, cos]])
    return jnp.asarray(ahead, BF16), jnp.asarray(back, BF16)


def mm(left, right):
    return jnp.dot(left, right, preferred_element_type=F32)


def body(sequence_in, value_proj, gate_proj, filter_response, skip_weight, output_proj):
    rows = sequence_in.shape[0]
    half = rows // 2
    my_y, my_x, my_zl, my_c = (lax.axis_index(a) for a in ("y", "x", "zl", "c"))
    at = jnp.stack([my_y, my_x, my_c, my_zl])

    act = lax.dynamic_slice(sequence_in, (my_c * half, 0), (half, sequence_in.shape[1]))
    act = lax.all_gather(act, ("x", "c"), axis=0, tiled=True)

    resp = filter_response[:, :, 0, :].reshape(2, rows, 4, 16, 16)
    resp = resp.transpose(3, 2, 4, 0, 1).reshape(64, 16, 2 * rows)

    w_y, g_y = spread(value_proj, gate_proj)
    w_y, resp = tie(w_y, resp)
    w_all = [lax.ppermute(w_y, "y", shift(step)) if step else w_y for step in range(4)]
    resp = lax.all_to_all(resp, SEQ, 0, 0, tiled=True)
    *w_all, resp = tie(*w_all, resp)
    value = project(my_y, act, w_all)
    g_all = lax.all_gather(g_y, "y", axis=0, tiled=True)
    full = rows * 64

    slabs = lax.all_to_all(value, SLABS, 0, 0, tiled=True)
    slabs = slabs.reshape(64, 16, rows)

    resp = resp.astype(F32)
    s_idx = lax.iota(jnp.int32, 64)
    k_idx = lax.iota(jnp.int32, 64)

    def slab_table(order):
        angle = (k_idx[:, None] * order[None, :] % 64).astype(F32) * (2.0 * math.pi / 64)
        return jnp.concatenate([jnp.cos(angle), -jnp.sin(angle)])

    first = slab_table(s_idx).astype(BF16)
    last = (slab_table(s_idx) / full).astype(BF16)
    r_idx = lax.iota(jnp.int32, rows)
    twist = (k_idx[:, None] * r_idx[None, :]).astype(F32) * (2.0 * math.pi / full)
    t_cos, t_sin = jnp.cos(twist)[:, None, :], jnp.sin(twist)[:, None, :]
    ahead, back = inner_tables(rows)

    sect = jnp.einsum("ks,scr->kcr", first, slabs, preferred_element_type=F32)
    re, im = sect[:64], sect[64:]
    turned = jnp.concatenate([re * t_cos + im * t_sin, im * t_cos - re * t_sin], axis=2)
    spec = mm(turned.astype(BF16), ahead)
    re, im = spec[..., :rows], spec[..., rows:]
    h_re, h_im = resp[..., :rows], resp[..., rows:]
    prod = jnp.concatenate([re * h_re - im * h_im, re * h_im + im * h_re], axis=2)
    inv = mm(prod.astype(BF16), back)
    re, im = inv[..., :rows], inv[..., rows:]
    reverted = jnp.concatenate([re * t_cos - im * t_sin, re * t_sin + im * t_cos], axis=0)
    conv = jnp.einsum("ks,kcr->scr", last, reverted.astype(BF16), preferred_element_type=F32)
    conv = lax.all_to_all(
        conv.astype(BF16).reshape(16, 4, 16, rows), SLABS, 0, 0, tiled=True
    )

    gate = project(my_y * 0, act, [g_all])
    skip = lax.dynamic_slice(skip_weight, (my_x * 256,), (256,)).reshape(16, 1, 16, 1)
    mixed = (gate.astype(F32) * (conv.astype(F32) + skip * value.astype(F32))).astype(BF16)

    pieces = []
    for step in range(4):
        piece = lax.dynamic_index_in_dim(mixed, (my_x + step) % 4, 1, keepdims=False)
        piece = piece.reshape(256, rows)
        pieces.append(lax.ppermute(piece, "x", shift(step)) if step else piece)

    home, give = home_and_give(at, pieces, output_proj)
    got = lax.ppermute(give, "c", SWAP)
    away, mine = keep(at, home, output_proj)
    got_away = lax.dynamic_index_in_dim(got, 1 - my_zl, 0, keepdims=False)
    got_mine = lax.dynamic_index_in_dim(got, my_zl, 0, keepdims=False)
    back = lax.ppermute((away + got_away.astype(F32)).astype(BF16), "zl", SWAP)
    return (mine + got_mine.astype(F32) + back.astype(F32)).astype(BF16)


def solution(mesh):
    fine = Mesh(mesh.devices.reshape(4, 4, 4, 2, 2), ("y", "zh", "x", "zl", "c"))
    tp = ("zl", "c")
    placed = (
        P(SEQ, None),
        P(SEQ, tp),
        P(SEQ, tp),
        P(None, None, SEQ, tp),
        P(tp),
        P(tp, None),
    )
    return jax.shard_map(
        body, mesh=fine, in_specs=placed, out_specs=P(SEQ, tp), check_vma=False
    )
```

```python
import math

import jax
import jax.numpy as jnp
import numpy as np
from jax import lax
from jax.experimental import pallas as pl
from jax.experimental.pallas import tpu as pltpu
from jax.sharding import Mesh
from jax.sharding import PartitionSpec as P

F32 = jnp.float32
BF16 = jnp.bfloat16
SEQ = ("y", "zh", "x")
SLABS = ("y", "zh")
SWAP = [(0, 1), (1, 0)]


def shift(count):
    return [(i, (i + count) % 4) for i in range(4)]


def tie(*arrays):
    return lax.optimization_barrier(arrays)


def in_hbm(arrays):
    return [pltpu.with_memory_space_constraint(a, pltpu.HBM) for a in arrays]


def turn_kernel(source, out):
    for part in range(4):
        block = source[:, part * 256 : (part + 1) * 256].astype(F32).T
        out[:, part] = block.astype(BF16).reshape(16, 16, block.shape[1])


def turn_filter(response):
    inside = pl.BlockSpec(memory_space=pltpu.VMEM)
    return pl.pallas_call(
        turn_kernel,
        out_shape=jax.ShapeDtypeStruct((16, 4, 16, response.shape[0]), BF16),
        in_specs=[inside],
        out_specs=inside,
    )(response)


def split_kernel(own_ref, first, second, *outs):
    rows = first.shape[0]
    for step, out in enumerate(outs):
        col = pl.multiple_of(lax.rem(own_ref[0] + step, 4) * 256, 128)
        out[:rows] = first[:, pl.ds(col, 256)]
        out[rows:] = second[:, pl.ds(col, 256)]


def split_columns(own, first, second):
    inside = pl.BlockSpec(memory_space=pltpu.VMEM)
    one = jax.ShapeDtypeStruct((2 * first.shape[0], 256), first.dtype)
    return pl.pallas_call(
        split_kernel,
        out_shape=(one,) * 4,
        in_specs=[pl.BlockSpec(memory_space=pltpu.SMEM), inside, inside],
        out_specs=(inside,) * 4,
    )(own.reshape(1), first, second)


def place_kernel(own_ref, *refs):
    sources, outs = refs[:4], refs[4:]
    rows = sources[0].shape[0] // len(outs)
    for step, source in enumerate(sources):
        row = pl.multiple_of(lax.rem(own_ref[0] + 4 - step, 4) * rows, 16)
        for at, out in enumerate(outs):
            out[pl.ds(row, rows)] = source[at * rows : (at + 1) * rows]


def place(own, pieces, count):
    inside = pl.BlockSpec(memory_space=pltpu.VMEM)
    rows, cols = pieces[0].shape
    one = jax.ShapeDtypeStruct((4 * rows // count, cols), pieces[0].dtype)
    return pl.pallas_call(
        place_kernel,
        out_shape=(one,) * count,
        in_specs=[pl.BlockSpec(memory_space=pltpu.SMEM)] + [inside] * 4,
        out_specs=(inside,) * count,
    )(own.reshape(1), *pieces)


def to_all(block, axis):
    return [lax.ppermute(block, axis, shift(step)) if step else block for step in range(4)]


def project_kernel(own_ref, act_ref, *refs):
    w_refs, (out, a_buf, w_buf, sems) = refs[:-4], refs[-4:]
    rows, block = a_buf.shape[1], w_buf.shape[0] // len(w_refs)
    copies = []
    for step, source in enumerate(w_refs):
        row = pl.multiple_of(lax.rem(own_ref[0] + 4 - step, 4) * block, 16)
        copies.append((source, w_buf.at[pl.ds(row, block)]))
    for part in range(4):
        copies.append((act_ref.at[pl.ds(part * rows, rows)], a_buf.at[part]))
    copies = [
        pltpu.make_async_copy(src, dst, sems.at[at]) for at, (src, dst) in enumerate(copies)
    ]
    for copy in copies:
        copy.start()
    for copy in copies[: len(w_refs)]:
        copy.wait()
    for part in range(4):
        copies[len(w_refs) + part].wait()
        prod = jnp.dot(a_buf[part], w_buf[...], preferred_element_type=F32)
        out[:, part] = prod.T.astype(BF16).reshape(16, 16, rows)


def project(own, act, weights):
    rows, depth = act.shape[0] // 4, act.shape[1]
    cols = weights[0].shape[1]
    count = len(weights) + 4
    return pl.pallas_call(
        project_kernel,
        out_shape=jax.ShapeDtypeStruct((16, 4, cols // 16, rows), BF16),
        in_specs=[pl.BlockSpec(memory_space=pltpu.SMEM)]
        + [pl.BlockSpec(memory_space=pltpu.HBM)] * (len(weights) + 1),
        out_specs=pl.BlockSpec(memory_space=pltpu.VMEM),
        scratch_shapes=[
            pltpu.VMEM((4, rows, depth), BF16),
            pltpu.VMEM((depth, cols), BF16),
            pltpu.SemaphoreType.DMA((count,)),
        ],
        compiler_params=pltpu.CompilerParams(vmem_limit_bytes=40 * 1024 * 1024),
    )(own.reshape(1), *in_hbm([act, *weights]))


def column_block(weight_ref, block, w_buf, sem):
    col = pl.multiple_of(block * w_buf.shape[1], 128)
    return pltpu.make_async_copy(weight_ref.at[:, pl.ds(col, w_buf.shape[1])], w_buf, sem)


def mix_kernel(at_ref, conv_ref, *refs):
    values, gates, refs = refs[:4], refs[4:8], refs[8:]
    skip_ref, weight_ref, home_ref, give_ref, w_buf, sem = refs
    own_x, own_c, own_z = at_ref[1], at_ref[2], at_ref[3]
    copy = column_block(weight_ref, 2 * (1 - own_z) + 1 - own_c, w_buf, sem)
    copy.start()
    rows = home_ref.shape[0]
    for step in range(4):
        src = lax.rem(own_x + 4 - step, 4)
        conv = conv_ref[:, src].astype(F32).reshape(256, rows)
        value = values[step][...].astype(F32).reshape(256, rows)
        gate = gates[step][...].astype(F32).reshape(256, rows)
        mixed = gate * (conv + skip_ref[src] * value)
        col = pl.multiple_of(src * 256, 128)
        home_ref[:, pl.ds(col, 256)] = mixed.T.astype(BF16)
    copy.wait()
    give_ref[...] = jnp.dot(home_ref[...], w_buf[...], preferred_element_type=F32).astype(BF16)


INSIDE = pl.BlockSpec(memory_space=pltpu.VMEM)
OUTSIDE = pl.BlockSpec(memory_space=pltpu.HBM)
SCALARS = pl.BlockSpec(memory_space=pltpu.SMEM)


def mix_and_give(at, conv, values, gates, skip, weight):
    rows = conv.shape[-1]
    one = jax.ShapeDtypeStruct((rows, 1024), BF16)
    return pl.pallas_call(
        mix_kernel,
        out_shape=(one, one),
        in_specs=[SCALARS] + [INSIDE] * 10 + [OUTSIDE],
        out_specs=(INSIDE, INSIDE),
        scratch_shapes=[pltpu.VMEM((1024, 1024), BF16), pltpu.SemaphoreType.DMA],
        compiler_params=pltpu.CompilerParams(vmem_limit_bytes=32 * 1024 * 1024),
    )(at, conv, *values, *gates, skip, *in_hbm([weight]))


def away_kernel(at_ref, home_ref, weight_ref, away_ref, w_buf, sem):
    copy = column_block(weight_ref, 2 * (1 - at_ref[3]) + at_ref[2], w_buf, sem)
    copy.start()
    copy.wait()
    away_ref[...] = jnp.dot(home_ref[...], w_buf[...], preferred_element_type=F32)


def away_part(at, home, weight):
    return pl.pallas_call(
        away_kernel,
        out_shape=jax.ShapeDtypeStruct((home.shape[0], 1024), F32),
        in_specs=[SCALARS, INSIDE, OUTSIDE],
        out_specs=INSIDE,
        scratch_shapes=[pltpu.VMEM((1024, 1024), BF16), pltpu.SemaphoreType.DMA],
        compiler_params=pltpu.CompilerParams(vmem_limit_bytes=24 * 1024 * 1024),
    )(at, home, *in_hbm([weight]))


def near_kernel(at_ref, home_ref, weight_ref, give_ref, mine_ref, w_buf, sems):
    own_z, own_c = at_ref[3], at_ref[2]
    copies = [
        column_block(weight_ref, 2 * own_z + core, w_buf.at[at], sems.at[at])
        for at, core in enumerate((1 - own_c, own_c))
    ]
    for copy in copies:
        copy.start()
    for at, out_ref in enumerate((give_ref, mine_ref)):
        copies[at].wait()
        out_ref[...] = jnp.dot(
            home_ref[...], w_buf[at], preferred_element_type=F32
        ).astype(out_ref.dtype)


def near_parts(at, home, weight):
    rows = home.shape[0]
    return pl.pallas_call(
        near_kernel,
        out_shape=(
            jax.ShapeDtypeStruct((rows, 1024), BF16),
            jax.ShapeDtypeStruct((rows, 1024), F32),
        ),
        in_specs=[SCALARS, INSIDE, OUTSIDE],
        out_specs=(INSIDE, INSIDE),
        scratch_shapes=[pltpu.VMEM((2, 1024, 1024), BF16), pltpu.SemaphoreType.DMA((2,))],
        compiler_params=pltpu.CompilerParams(vmem_limit_bytes=24 * 1024 * 1024),
    )(at, home, *in_hbm([weight]))


def inner_tables(count):
    idx = np.arange(count)
    angle = (idx[:, None] * idx[None, :] % count) * (2.0 * math.pi / count)
    cos, sin = np.cos(angle), np.sin(angle)
    ahead = np.block([[cos, -sin], [sin, cos]])
    back = np.block([[cos, sin], [-sin, cos]])
    return jnp.asarray(ahead, BF16), jnp.asarray(back, BF16)


def mm(left, right):
    return jnp.dot(left, right, preferred_element_type=F32)


def along_x(parts, own):
    pieces = []
    for step in range(4):
        piece = lax.dynamic_index_in_dim(parts, (own + step) % 4, 1, keepdims=False)
        pieces.append(lax.ppermute(piece, "x", shift(step)) if step else piece)
    return pieces


def body(sequence_in, value_proj, gate_proj, filter_response, skip_weight, output_proj):
    rows = sequence_in.shape[0]
    half = rows // 2
    my_y, my_x, my_zl, my_c = (lax.axis_index(a) for a in ("y", "x", "zl", "c"))
    at = jnp.stack([my_y, my_x, my_c, my_zl])

    act = lax.dynamic_slice(sequence_in, (my_c * half, 0), (half, sequence_in.shape[1]))
    act = lax.all_gather(act, ("x", "c"), axis=0, tiled=True)

    resp = turn_filter(filter_response.reshape(2 * rows, 1024)).reshape(64, 16, 2 * rows)

    wg = split_columns(my_x, value_proj, gate_proj)
    wg = [lax.ppermute(p, "x", shift(step)) if step else p for step, p in enumerate(wg)]
    resp, *wg = tie(resp, *wg)
    resp = lax.all_to_all(resp, SEQ, 0, 0, tiled=True)
    w_x, g_x = place(my_x, wg, 2)
    my_zh = lax.axis_index("zh")
    (w_y,) = place(my_zh, to_all(w_x, "zh"), 1)
    w_y, g_x = tie(w_y, g_x)
    w_all = to_all(w_y, "y")
    g_z = to_all(g_x, "zh")
    *w_all, g_z[1], g_z[2], g_z[3] = tie(*w_all, *g_z[1:])
    (g_y,) = place(my_zh, g_z, 1)
    g_all = lax.all_gather(g_y, "y", axis=0, tiled=True)
    value = project(my_y, act, w_all)
    value, resp = tie(value, resp)
    full = rows * 64

    slabs = lax.all_to_all(value, SLABS, 0, 0, tiled=True)
    values = along_x(value, my_x)
    slabs, g_all, *values = tie(slabs, g_all, *values)
    slabs = slabs.reshape(64, 16, rows)

    s_idx = lax.iota(jnp.int32, 64)
    k_idx = lax.iota(jnp.int32, 64)

    def slab_table(order):
        angle = (k_idx[:, None] * order[None, :] % 64).astype(F32) * (2.0 * math.pi / 64)
        return jnp.concatenate([jnp.cos(angle), -jnp.sin(angle)])

    first = slab_table(s_idx).astype(BF16)
    last = (slab_table(s_idx) / full).astype(BF16)
    r_idx = lax.iota(jnp.int32, rows)
    twist = (k_idx[:, None] * r_idx[None, :]).astype(F32) * (2.0 * math.pi / full)
    t_cos, t_sin = jnp.cos(twist)[:, None, :], jnp.sin(twist)[:, None, :]
    ahead, back = inner_tables(rows)

    sect = jnp.einsum("ks,scr->kcr", first, slabs, preferred_element_type=F32)
    re, im = sect[:64], sect[64:]
    turned = jnp.concatenate([re * t_cos + im * t_sin, im * t_cos - re * t_sin], axis=2)
    spec = mm(turned.astype(BF16), ahead)
    re, im = spec[..., :rows], spec[..., rows:]
    resp = resp.astype(F32)
    h_re, h_im = resp[..., :rows], resp[..., rows:]
    prod = jnp.concatenate([re * h_re - im * h_im, re * h_im + im * h_re], axis=2)
    inv = mm(prod.astype(BF16), back)
    re, im = inv[..., :rows], inv[..., rows:]
    reverted = jnp.concatenate([re * t_cos - im * t_sin, re * t_sin + im * t_cos], axis=0)
    conv = jnp.einsum("ks,kcr->scr", last, reverted.astype(BF16), preferred_element_type=F32)
    conv = lax.all_to_all(conv.astype(BF16), SEQ, 0, 0, tiled=True).reshape(16, 4, 16, rows)
    gate = project(my_y * 0, act, [g_all])
    gates = along_x(gate, my_x)

    home, give = mix_and_give(
        at, conv, values, gates, skip_weight.reshape(4, 256, 1), output_proj
    )
    got = lax.ppermute(give, "c", SWAP)
    away = away_part(at, home, output_proj)
    away = (away + got.astype(F32)).astype(BF16)
    back = lax.ppermute(away, "zl", SWAP)
    home, away = tie(home, away)
    give, mine = near_parts(at, home, output_proj)
    mine = mine + lax.ppermute(give, "c", SWAP).astype(F32)
    return (mine + back.astype(F32)).astype(BF16)


def solution(mesh):
    fine = Mesh(mesh.devices.reshape(4, 4, 4, 2, 2), ("y", "zh", "x", "zl", "c"))
    tp = ("zl", "c")
    placed = (
        P(SEQ, None),
        P(SEQ, tp),
        P(SEQ, tp),
        P(None, None, SEQ, tp),
        P(tp),
        P(tp, None),
    )
    return jax.shard_map(
        body, mesh=fine, in_specs=placed, out_specs=P(SEQ, tp), check_vma=False
    )
```

```python
import math

import jax
import jax.numpy as jnp
import numpy as np
from jax import lax
from jax.experimental import pallas as pl
from jax.experimental.pallas import tpu as pltpu
from jax.sharding import Mesh
from jax.sharding import PartitionSpec as P

F32 = jnp.float32
BF16 = jnp.bfloat16
SEQ = ("y", "zh", "x")
SLABS = ("y", "zh")
SWAP = [(0, 1), (1, 0)]
INSIDE = pl.BlockSpec(memory_space=pltpu.VMEM)
OUTSIDE = pl.BlockSpec(memory_space=pltpu.HBM)
SCALARS = pl.BlockSpec(memory_space=pltpu.SMEM)


def shift(count):
    return [(i, (i + count) % 4) for i in range(4)]


def tie(*arrays):
    return lax.optimization_barrier(arrays)


def in_hbm(arrays):
    return [pltpu.with_memory_space_constraint(a, pltpu.HBM) for a in arrays]


def turn_kernel(source, out):
    for part in range(4):
        block = source[:, part * 256 : (part + 1) * 256].astype(F32).T
        out[:, part] = block.astype(BF16).reshape(16, 16, block.shape[1])


def turn_filter(response):
    inside = pl.BlockSpec(memory_space=pltpu.VMEM)
    return pl.pallas_call(
        turn_kernel,
        out_shape=jax.ShapeDtypeStruct((16, 4, 16, response.shape[0]), BF16),
        in_specs=[inside],
        out_specs=inside,
    )(response)


def split_kernel(own_ref, first, second, *outs):
    rows = first.shape[0]
    for step, out in enumerate(outs):
        col = pl.multiple_of(lax.rem(own_ref[0] + step, 4) * 256, 128)
        out[:rows] = first[:, pl.ds(col, 256)]
        out[rows:] = second[:, pl.ds(col, 256)]


def split_columns(own, first, second):
    inside = pl.BlockSpec(memory_space=pltpu.VMEM)
    one = jax.ShapeDtypeStruct((2 * first.shape[0], 256), first.dtype)
    return pl.pallas_call(
        split_kernel,
        out_shape=(one,) * 4,
        in_specs=[pl.BlockSpec(memory_space=pltpu.SMEM), inside, inside],
        out_specs=(inside,) * 4,
    )(own.reshape(1), first, second)


def place_kernel(own_ref, *refs):
    sources, outs = refs[:4], refs[4:]
    rows = sources[0].shape[0] // len(outs)
    for step, source in enumerate(sources):
        row = pl.multiple_of(lax.rem(own_ref[0] + 4 - step, 4) * rows, 16)
        for at, out in enumerate(outs):
            out[pl.ds(row, rows)] = source[at * rows : (at + 1) * rows]


def place(own, pieces, count):
    inside = pl.BlockSpec(memory_space=pltpu.VMEM)
    rows, cols = pieces[0].shape
    one = jax.ShapeDtypeStruct((4 * rows // count, cols), pieces[0].dtype)
    return pl.pallas_call(
        place_kernel,
        out_shape=(one,) * count,
        in_specs=[pl.BlockSpec(memory_space=pltpu.SMEM)] + [inside] * 4,
        out_specs=(inside,) * count,
    )(own.reshape(1), *pieces)


def to_all(block, axis):
    return [lax.ppermute(block, axis, shift(step)) if step else block for step in range(4)]


def project_kernel(whole, at_ref, act_ref, *refs):
    a_buf, w_buf, sems = refs[-3:]
    outs = refs[-8:-3] if whole else refs[-7:-3]
    w_refs = refs[: len(refs) - 3 - len(outs)]
    rows, block = a_buf.shape[1], w_buf.shape[0] // len(w_refs)
    own_y, own_x = at_ref[0], at_ref[1]
    copies = []
    for step, source in enumerate(w_refs):
        row = pl.multiple_of(lax.rem(own_y + 4 - step, 4) * block, 16)
        copies.append((source, w_buf.at[pl.ds(row, block)]))
    parts = [lax.rem(own_x + step, 4) for step in range(4)]
    for step, part in enumerate(parts):
        row = pl.multiple_of(part * rows, 16)
        copies.append((act_ref.at[pl.ds(row, rows)], a_buf.at[step]))
    copies = [
        pltpu.make_async_copy(src, dst, sems.at[at]) for at, (src, dst) in enumerate(copies)
    ]
    for copy in copies:
        copy.start()
    for copy in copies[: len(w_refs)]:
        copy.wait()
    for step, part in enumerate(parts):
        copies[len(w_refs) + step].wait()
        prod = jnp.dot(a_buf[step], w_buf[...], preferred_element_type=F32).T.astype(BF16)
        outs[step][...] = prod
        if whole:
            outs[4][:, part] = prod.reshape(16, 16, rows)


def project(at, act, weights, whole):
    rows, depth = act.shape[0] // 4, act.shape[1]
    cols = weights[0].shape[1]
    count = len(weights) + 4
    shapes = [(cols, rows)] * 4 + [(16, 4, cols // 16, rows)] * whole
    return pl.pallas_call(
        lambda *refs: project_kernel(whole, *refs),
        out_shape=[jax.ShapeDtypeStruct(shape, BF16) for shape in shapes],
        in_specs=[SCALARS] + [OUTSIDE] * (len(weights) + 1),
        out_specs=[INSIDE] * len(shapes),
        scratch_shapes=[
            pltpu.VMEM((4, rows, depth), BF16),
            pltpu.VMEM((depth, cols), BF16),
            pltpu.SemaphoreType.DMA((count,)),
        ],
        compiler_params=pltpu.CompilerParams(vmem_limit_bytes=40 * 1024 * 1024),
    )(at, *in_hbm([act, *weights]))


def fetch(sources, buffers, sems):
    copies = [
        pltpu.make_async_copy(src, dst, sems.at[at])
        for at, (src, dst) in enumerate(zip(sources, buffers))
    ]
    for copy in copies:
        copy.start()
    return copies


def column_block(weight_ref, block, w_buf, sem):
    col = pl.multiple_of(block * w_buf.shape[1], 128)
    return pltpu.make_async_copy(weight_ref.at[:, pl.ds(col, w_buf.shape[1])], w_buf, sem)


def mix_kernel(at_ref, skip_ref, conv_hbm, *refs):
    sources, weight_ref = (conv_hbm,) + refs[:8], refs[8]
    home_ref, give_ref, conv_buf, vg_buf, w_buf, sem, sems = refs[9:]
    own_x, own_c, own_z = at_ref[1], at_ref[2], at_ref[3]
    copies = fetch(sources, [conv_buf] + [vg_buf.at[at] for at in range(8)], sems)
    copy = column_block(weight_ref, 2 * (1 - own_z) + 1 - own_c, w_buf, sem)
    copy.start()
    rows = home_ref.shape[0]
    for other in copies:
        other.wait()
    for step in range(4):
        src = lax.rem(own_x + 4 - step, 4)
        conv = conv_buf[:, src].astype(F32).reshape(256, rows)
        value, gate = vg_buf[step].astype(F32), vg_buf[4 + step].astype(F32)
        mixed = gate * (conv + skip_ref[src] * value)
        col = pl.multiple_of(src * 256, 128)
        home_ref[:, pl.ds(col, 256)] = mixed.T.astype(BF16)
    copy.wait()
    give_ref[...] = jnp.dot(home_ref[...], w_buf[...], preferred_element_type=F32).astype(BF16)


def mix_and_give(at, conv, values, gates, skip, weight):
    rows = conv.shape[-1]
    one = jax.ShapeDtypeStruct((rows, 1024), BF16)
    return pl.pallas_call(
        mix_kernel,
        out_shape=(one, one),
        in_specs=[SCALARS, INSIDE] + [OUTSIDE] * 10,
        out_specs=(INSIDE, INSIDE),
        scratch_shapes=[
            pltpu.VMEM(conv.shape, BF16),
            pltpu.VMEM((8, 256, rows), BF16),
            pltpu.VMEM((1024, 1024), BF16),
            pltpu.SemaphoreType.DMA,
            pltpu.SemaphoreType.DMA((9,)),
        ],
        compiler_params=pltpu.CompilerParams(vmem_limit_bytes=32 * 1024 * 1024),
    )(at, skip, *in_hbm([conv, *values, *gates, weight]))


def away_kernel(at_ref, home_ref, weight_ref, away_ref, w_buf, sem):
    copy = column_block(weight_ref, 2 * (1 - at_ref[3]) + at_ref[2], w_buf, sem)
    copy.start()
    copy.wait()
    away_ref[...] = jnp.dot(home_ref[...], w_buf[...], preferred_element_type=F32)


def away_part(at, home, weight):
    return pl.pallas_call(
        away_kernel,
        out_shape=jax.ShapeDtypeStruct((home.shape[0], 1024), F32),
        in_specs=[SCALARS, INSIDE, OUTSIDE],
        out_specs=INSIDE,
        scratch_shapes=[pltpu.VMEM((1024, 1024), BF16), pltpu.SemaphoreType.DMA],
        compiler_params=pltpu.CompilerParams(vmem_limit_bytes=24 * 1024 * 1024),
    )(at, home, *in_hbm([weight]))


def near_kernel(at_ref, home_ref, weight_ref, give_ref, mine_ref, w_buf, sems):
    own_z, own_c = at_ref[3], at_ref[2]
    copies = [
        column_block(weight_ref, 2 * own_z + core, w_buf.at[at], sems.at[at])
        for at, core in enumerate((1 - own_c, own_c))
    ]
    for copy in copies:
        copy.start()
    for at, out_ref in enumerate((give_ref, mine_ref)):
        copies[at].wait()
        out_ref[...] = jnp.dot(
            home_ref[...], w_buf[at], preferred_element_type=F32
        ).astype(out_ref.dtype)


def near_parts(at, home, weight):
    rows = home.shape[0]
    return pl.pallas_call(
        near_kernel,
        out_shape=(
            jax.ShapeDtypeStruct((rows, 1024), BF16),
            jax.ShapeDtypeStruct((rows, 1024), F32),
        ),
        in_specs=[SCALARS, INSIDE, OUTSIDE],
        out_specs=(INSIDE, INSIDE),
        scratch_shapes=[pltpu.VMEM((2, 1024, 1024), BF16), pltpu.SemaphoreType.DMA((2,))],
        compiler_params=pltpu.CompilerParams(vmem_limit_bytes=24 * 1024 * 1024),
    )(at, home, *in_hbm([weight]))


def tables(rows):
    slab = np.arange(64)
    angle = (slab[:, None] * slab[None, :] % 64) * (2.0 * math.pi / 64)
    first = np.concatenate([np.cos(angle), -np.sin(angle)])
    idx = np.arange(rows)
    angle = slab[:, None] * idx[None, :] * (2.0 * math.pi / (64 * rows))
    turn = np.stack([np.cos(angle), np.sin(angle)])
    angle = (idx[:, None] * idx[None, :] % rows) * (2.0 * math.pi / rows)
    cos, sin = np.cos(angle), np.sin(angle)
    ahead = np.block([[cos, -sin], [sin, cos]])
    back = np.block([[cos, sin], [-sin, cos]])
    last = first.T / (64 * rows)
    return (
        jnp.asarray(first, BF16),
        jnp.asarray(last, BF16),
        jnp.asarray(turn, F32),
        jnp.asarray(ahead, BF16),
        jnp.asarray(back, BF16),
    )


def mm(left, right):
    return jnp.dot(left, right, preferred_element_type=F32)


def filter_kernel(first, last, turn, *refs):
    sources, out_ref, x_buf, h_buf = refs[:4], refs[4], refs[5], refs[6]
    buffers, sems = refs[7:11], refs[11]
    slab_ref, resp_ref, ahead, back = buffers
    for copy in fetch(sources, buffers, sems):
        copy.wait()
    rows = slab_ref.shape[1]
    for ref, buf in ((slab_ref, x_buf), (resp_ref, h_buf)):
        for part in range(buf.shape[0]):
            buf[part] = ref[:, part * 128 : (part + 1) * 128].astype(F32)

    def pick_rows(buf, pick):
        return jnp.concatenate([buf[part, pick, :] for part in range(buf.shape[0])], axis=1)

    t_cos, t_sin = turn[0], turn[1]
    group = 4
    for start in range(0, 16, group):
        picks = [pl.ds(start + at, 64, stride=16) for at in range(group)]
        turned = []
        for pick in picks:
            sect = mm(first[...], pick_rows(x_buf, pick).astype(BF16))
            re, im = sect[:64], sect[64:]
            turned.append(
                jnp.concatenate([re * t_cos + im * t_sin, im * t_cos - re * t_sin], axis=1)
            )
        spec = mm(jnp.concatenate(turned).astype(BF16), ahead[...])
        prods = []
        for at, pick in enumerate(picks):
            re, im = spec[at * 64 : (at + 1) * 64, :rows], spec[at * 64 : (at + 1) * 64, rows:]
            resp = pick_rows(h_buf, pick)
            h_re, h_im = resp[:, :rows], resp[:, rows:]
            prods.append(
                jnp.concatenate([re * h_re - im * h_im, re * h_im + im * h_re], axis=1)
            )
        inv = mm(jnp.concatenate(prods).astype(BF16), back[...])
        for at, pick in enumerate(picks):
            re, im = inv[at * 64 : (at + 1) * 64, :rows], inv[at * 64 : (at + 1) * 64, rows:]
            reverted = jnp.concatenate([re * t_cos - im * t_sin, re * t_sin + im * t_cos])
            conv = mm(last[...], reverted.astype(BF16))
            for part in range(x_buf.shape[0]):
                x_buf[part, pick, :] = conv[:, part * 128 : (part + 1) * 128]
    for part in range(x_buf.shape[0]):
        out_ref[:, part * 128 : (part + 1) * 128] = x_buf[part].astype(BF16)


def filtered(slabs, resp):
    count, rows = slabs.shape
    first, last, turn, ahead, back = tables(rows)
    return pl.pallas_call(
        filter_kernel,
        out_shape=jax.ShapeDtypeStruct((count, rows), BF16),
        in_specs=[INSIDE] * 3 + [OUTSIDE] * 4,
        out_specs=INSIDE,
        scratch_shapes=[
            pltpu.VMEM((rows // 128, count, 128), F32),
            pltpu.VMEM((2 * rows // 128, count, 128), F32),
            pltpu.VMEM((count, rows), BF16),
            pltpu.VMEM((count, 2 * rows), BF16),
            pltpu.VMEM((2 * rows, 2 * rows), BF16),
            pltpu.VMEM((2 * rows, 2 * rows), BF16),
            pltpu.SemaphoreType.DMA((4,)),
        ],
        compiler_params=pltpu.CompilerParams(vmem_limit_bytes=32 * 1024 * 1024),
    )(first, last, turn, *in_hbm([slabs, resp, ahead, back]))


def along_x(pieces):
    return [lax.ppermute(p, "x", shift(step)) if step else p for step, p in enumerate(pieces)]


def body(sequence_in, value_proj, gate_proj, filter_response, skip_weight, output_proj):
    rows = sequence_in.shape[0]
    half = rows // 2
    my_y, my_x, my_zl, my_c = (lax.axis_index(a) for a in ("y", "x", "zl", "c"))
    at = jnp.stack([my_y, my_x, my_c, my_zl])

    resp = turn_filter(filter_response.reshape(2 * rows, 1024))
    resp, ahead_x, ahead_c = tie(resp, my_x, my_c)
    resp = lax.all_to_all(resp.reshape(64, 16, 2 * rows), SEQ, 0, 0, tiled=True)

    wg = split_columns(ahead_x, value_proj, gate_proj)
    wg = [lax.ppermute(p, "x", shift(step)) if step else p for step, p in enumerate(wg)]
    w_x, g_x = place(my_x, wg, 2)
    my_zh = lax.axis_index("zh")

    act = lax.dynamic_slice(sequence_in, (ahead_c * half, 0), (half, sequence_in.shape[1]))
    act = lax.all_gather(act, ("x", "c"), axis=0, tiled=True)

    (w_y,) = place(my_zh, to_all(w_x, "zh"), 1)
    w_y, g_x = tie(w_y, g_x)
    w_all = to_all(w_y, "y")
    (g_y,) = place(my_zh, to_all(g_x, "zh"), 1)
    *w_all, resp, g_y = tie(*w_all, resp, g_y)
    g_all = lax.all_gather(g_y, "y", axis=0, tiled=True)
    *values, value = project(at, act, w_all, True)
    slabs = lax.all_to_all(value, SLABS, 0, 0, tiled=True)
    values = along_x(values)
    slabs, *values = tie(slabs, *values)
    conv = filtered(slabs.reshape(1024, rows), resp.reshape(1024, 2 * rows))
    conv = conv.reshape(64, 16, rows)
    conv = lax.all_to_all(conv, SEQ, 0, 0, tiled=True).reshape(16, 4, 16, rows)
    gates = along_x(project(at * jnp.array([0, 1, 0, 0], jnp.int32), act, [g_all], False))

    home, give = mix_and_give(
        at, conv, values, gates, skip_weight.reshape(4, 256, 1), output_proj
    )
    got = lax.ppermute(give, "c", SWAP)
    away = away_part(at, home, output_proj)
    away = (away + got.astype(F32)).astype(BF16)
    back = lax.ppermute(away, "zl", SWAP)
    home, away = tie(home, away)
    give, mine = near_parts(at, home, output_proj)
    mine = mine + lax.ppermute(give, "c", SWAP).astype(F32)
    return (mine + back.astype(F32)).astype(BF16)


def solution(mesh):
    fine = Mesh(mesh.devices.reshape(4, 4, 4, 2, 2), ("y", "zh", "x", "zl", "c"))
    tp = ("zl", "c")
    placed = (
        P(SEQ, None),
        P(SEQ, tp),
        P(SEQ, tp),
        P(None, None, SEQ, tp),
        P(tp),
        P(tp, None),
    )
    return jax.shard_map(
        body, mesh=fine, in_specs=placed, out_specs=P(SEQ, tp), check_vma=False
    )
```

```python
import math

import jax
import jax.numpy as jnp
import numpy as np
from jax import lax
from jax.experimental import pallas as pl
from jax.experimental.pallas import tpu as pltpu
from jax.sharding import Mesh
from jax.sharding import PartitionSpec as P

F32 = jnp.float32
BF16 = jnp.bfloat16
SEQ = ("y", "zh", "x")
SLABS = ("y", "zh")
SWAP = [(0, 1), (1, 0)]
INSIDE = pl.BlockSpec(memory_space=pltpu.VMEM)
OUTSIDE = pl.BlockSpec(memory_space=pltpu.HBM)
SCALARS = pl.BlockSpec(memory_space=pltpu.SMEM)


def shift(count):
    return [(i, (i + count) % 4) for i in range(4)]


def tie(*arrays):
    return lax.optimization_barrier(arrays)


def in_hbm(arrays):
    return [pltpu.with_memory_space_constraint(a, pltpu.HBM) for a in arrays]


def in_vmem(arrays):
    return [pltpu.with_memory_space_constraint(a, pltpu.VMEM) for a in arrays]


def turn_kernel(source, out):
    for part in range(4):
        block = source[:, part * 256 : (part + 1) * 256].astype(F32).T
        out[:, part] = block.astype(BF16).reshape(16, 16, block.shape[1])


def turn_filter(response):
    inside = pl.BlockSpec(memory_space=pltpu.VMEM)
    return pl.pallas_call(
        turn_kernel,
        out_shape=jax.ShapeDtypeStruct((16, 4, 16, response.shape[0]), BF16),
        in_specs=[inside],
        out_specs=inside,
    )(response)


def split_kernel(own_ref, first, second, *outs):
    rows = first.shape[0]
    for step, out in enumerate(outs):
        col = pl.multiple_of(lax.rem(own_ref[0] + step, 4) * 256, 128)
        out[:rows] = first[:, pl.ds(col, 256)]
        out[rows:] = second[:, pl.ds(col, 256)]


def split_columns(own, first, second):
    inside = pl.BlockSpec(memory_space=pltpu.VMEM)
    one = jax.ShapeDtypeStruct((2 * first.shape[0], 256), first.dtype)
    return pl.pallas_call(
        split_kernel,
        out_shape=(one,) * 4,
        in_specs=[pl.BlockSpec(memory_space=pltpu.SMEM), inside, inside],
        out_specs=(inside,) * 4,
    )(own.reshape(1), first, second)


def place_kernel(own_ref, *refs):
    sources, outs = refs[:4], refs[4:]
    rows = sources[0].shape[0] // len(outs)
    for step, source in enumerate(sources):
        row = pl.multiple_of(lax.rem(own_ref[0] + 4 - step, 4) * rows, 16)
        for at, out in enumerate(outs):
            out[pl.ds(row, rows)] = source[at * rows : (at + 1) * rows]


def place(own, pieces, count):
    inside = pl.BlockSpec(memory_space=pltpu.VMEM)
    rows, cols = pieces[0].shape
    one = jax.ShapeDtypeStruct((4 * rows // count, cols), pieces[0].dtype)
    return pl.pallas_call(
        place_kernel,
        out_shape=(one,) * count,
        in_specs=[pl.BlockSpec(memory_space=pltpu.SMEM)] + [inside] * 4,
        out_specs=(inside,) * count,
    )(own.reshape(1), *in_vmem(pieces))


def to_all(block, axis):
    return [lax.ppermute(block, axis, shift(step)) if step else block for step in range(4)]


def sum_kernel(steps, at_ref, act_ref, *refs):
    w_refs, (total, a_buf, w_buf, sems) = refs[: len(steps)], refs[len(steps) :]
    depth = w_buf.shape[1]
    copies = []
    for at, step in enumerate(steps):
        first = pl.multiple_of(lax.rem(at_ref[0] + 4 - step, 4) * depth, depth)
        pair = (w_refs[at], act_ref.at[:, pl.ds(first, depth)])
        copies.append(fetch(pair, (w_buf.at[at], a_buf.at[at]), sems.at[at]))
    for at, pair in enumerate(copies):
        for copy in pair:
            copy.wait()
        prod = jnp.dot(a_buf[at], w_buf[at], preferred_element_type=F32)
        total[...] = prod if at == 0 else total[...] + prod


def part_sum(at, act, weights, steps):
    rows, depth = act.shape[0], act.shape[1] // 4
    cols = weights[0].shape[1]
    return pl.pallas_call(
        lambda *refs: sum_kernel(steps, *refs),
        out_shape=jax.ShapeDtypeStruct((rows, cols), F32),
        in_specs=[SCALARS] + [OUTSIDE] * (len(steps) + 1),
        out_specs=INSIDE,
        scratch_shapes=[
            pltpu.VMEM((len(steps), rows, depth), BF16),
            pltpu.VMEM((len(steps), depth, cols), BF16),
            pltpu.SemaphoreType.DMA((len(steps), 2)),
        ],
        compiler_params=pltpu.CompilerParams(vmem_limit_bytes=40 * 1024 * 1024),
    )(at, *in_hbm([act, *weights]))


def finish_kernel(steps, whole, at_ref, act_ref, w_ref, *refs):
    a_buf, w_buf, total, sems = refs[-4:]
    outs = refs[-9:-4] if whole else refs[-8:-4]
    depth, rows = w_buf.shape[1], total.shape[0] // 4
    own_y, own_x = at_ref[0], at_ref[1]
    copies = []
    for at, step in enumerate(steps):
        first = pl.multiple_of(lax.rem(own_y + 4 - step, 4) * depth, depth)
        source = w_ref if len(steps) == 1 else w_ref.at[pl.ds(first, depth)]
        pair = (source, act_ref.at[:, pl.ds(first, depth)])
        copies.append(fetch(pair, (w_buf.at[at], a_buf.at[at]), sems.at[at]))
    has_sum = len(refs) > len(outs) + 4
    if has_sum:
        copies[0] += fetch(refs[:1], (total,), sems.at[len(steps)])
    for at, pair in enumerate(copies):
        for copy in pair:
            copy.wait()
        prod = jnp.dot(a_buf[at], w_buf[at], preferred_element_type=F32)
        total[...] = total[...] + prod if at or has_sum else prod
    for step in range(4):
        part = lax.rem(own_x + step, 4)
        row = pl.multiple_of(part * rows, 8)
        block = total[pl.ds(row, rows), :].T.astype(BF16)
        outs[step][...] = block
        if whole:
            outs[4][:, part] = block.reshape(16, 16, rows)


def project(at, act, weight, steps, before, whole):
    rows, depth = act.shape[0] // 4, act.shape[1] // 4
    cols = weight.shape[1]
    shapes = [(cols, rows)] * 4 + [(16, 4, cols // 16, rows)] * whole
    return pl.pallas_call(
        lambda *refs: finish_kernel(steps, whole, *refs),
        out_shape=[jax.ShapeDtypeStruct(shape, BF16) for shape in shapes],
        in_specs=[SCALARS] + [OUTSIDE] * (2 + len(before)),
        out_specs=[INSIDE] * len(shapes),
        scratch_shapes=[
            pltpu.VMEM((len(steps), 4 * rows, depth), BF16),
            pltpu.VMEM((len(steps), depth, cols), BF16),
            pltpu.VMEM((4 * rows, cols), F32),
            pltpu.SemaphoreType.DMA((len(steps) + 1, 2)),
        ],
        compiler_params=pltpu.CompilerParams(vmem_limit_bytes=40 * 1024 * 1024),
    )(at, *in_hbm([act, weight, *before]))


def fetch(sources, buffers, sems):
    copies = [
        pltpu.make_async_copy(src, dst, sems.at[at])
        for at, (src, dst) in enumerate(zip(sources, buffers))
    ]
    for copy in copies:
        copy.start()
    return copies


def column_block(weight_ref, block, w_buf, sem):
    col = pl.multiple_of(block * w_buf.shape[1], 128)
    return pltpu.make_async_copy(weight_ref.at[:, pl.ds(col, w_buf.shape[1])], w_buf, sem)


def mix_kernel(at_ref, skip_ref, weight_ref, conv_ref, value_ref, gate_ref, *refs):
    sources, (home_ref, give_ref, w_buf, sem, vg_buf, sems) = refs[:6], refs[6:]
    pieces = [vg_buf.at[at] for at in range(6)]
    others = fetch(sources, pieces, sems)
    values, gates = [value_ref] + pieces[:3], [gate_ref] + pieces[3:]
    own_x, own_c, own_z = at_ref[1], at_ref[2], at_ref[3]
    copy = column_block(weight_ref, 2 * (1 - own_z) + 1 - own_c, w_buf, sem)
    copy.start()
    rows = home_ref.shape[0]
    for step in range(4):
        if step == 1:
            for other in others:
                other.wait()
        src = lax.rem(own_x + 4 - step, 4)
        conv = conv_ref[:, src].astype(F32).reshape(256, rows)
        value, gate = values[step][...].astype(F32), gates[step][...].astype(F32)
        mixed = gate * (conv + skip_ref[src] * value)
        col = pl.multiple_of(src * 256, 128)
        home_ref[:, pl.ds(col, 256)] = mixed.T.astype(BF16)
    copy.wait()
    give_ref[...] = jnp.dot(home_ref[...], w_buf[...], preferred_element_type=F32).astype(BF16)


def mix_and_give(at, conv, values, gates, skip, weight):
    rows = conv.shape[-1]
    one = jax.ShapeDtypeStruct((rows, 1024), BF16)
    return pl.pallas_call(
        mix_kernel,
        out_shape=(one, one),
        in_specs=[SCALARS, INSIDE, OUTSIDE] + [INSIDE] * 3 + [OUTSIDE] * 6,
        out_specs=(INSIDE, INSIDE),
        scratch_shapes=[
            pltpu.VMEM((1024, 1024), BF16),
            pltpu.SemaphoreType.DMA,
            pltpu.VMEM((6, 256, rows), BF16),
            pltpu.SemaphoreType.DMA((6,)),
        ],
        compiler_params=pltpu.CompilerParams(vmem_limit_bytes=32 * 1024 * 1024),
    )(
        at,
        skip,
        *in_hbm([weight]),
        *in_vmem([conv, values[0], gates[0]]),
        *in_hbm([*values[1:], *gates[1:]]),
    )


def away_kernel(at_ref, home_ref, weight_ref, away_ref, w_buf, sem):
    copy = column_block(weight_ref, 2 * (1 - at_ref[3]) + at_ref[2], w_buf, sem)
    copy.start()
    copy.wait()
    away_ref[...] = jnp.dot(home_ref[...], w_buf[...], preferred_element_type=F32)


def away_part(at, home, weight):
    return pl.pallas_call(
        away_kernel,
        out_shape=jax.ShapeDtypeStruct((home.shape[0], 1024), F32),
        in_specs=[SCALARS, INSIDE, OUTSIDE],
        out_specs=INSIDE,
        scratch_shapes=[pltpu.VMEM((1024, 1024), BF16), pltpu.SemaphoreType.DMA],
        compiler_params=pltpu.CompilerParams(vmem_limit_bytes=24 * 1024 * 1024),
    )(at, home, *in_hbm([weight]))


def near_kernel(at_ref, home_ref, weight_ref, give_ref, mine_ref, w_buf, sems):
    own_z, own_c = at_ref[3], at_ref[2]
    copies = [
        column_block(weight_ref, 2 * own_z + core, w_buf.at[at], sems.at[at])
        for at, core in enumerate((1 - own_c, own_c))
    ]
    for copy in copies:
        copy.start()
    for at, out_ref in enumerate((give_ref, mine_ref)):
        copies[at].wait()
        out_ref[...] = jnp.dot(
            home_ref[...], w_buf[at], preferred_element_type=F32
        ).astype(out_ref.dtype)


def near_parts(at, home, weight):
    rows = home.shape[0]
    return pl.pallas_call(
        near_kernel,
        out_shape=(
            jax.ShapeDtypeStruct((rows, 1024), BF16),
            jax.ShapeDtypeStruct((rows, 1024), F32),
        ),
        in_specs=[SCALARS, INSIDE, OUTSIDE],
        out_specs=(INSIDE, INSIDE),
        scratch_shapes=[pltpu.VMEM((2, 1024, 1024), BF16), pltpu.SemaphoreType.DMA((2,))],
        compiler_params=pltpu.CompilerParams(vmem_limit_bytes=24 * 1024 * 1024),
    )(at, home, *in_hbm([weight]))


def tables(rows):
    slab = np.arange(64)
    angle = (slab[:, None] * slab[None, :] % 64) * (2.0 * math.pi / 64)
    first = np.concatenate([np.cos(angle), -np.sin(angle)])
    idx = np.arange(rows)
    angle = slab[:, None] * idx[None, :] * (2.0 * math.pi / (64 * rows))
    turn = np.stack([np.cos(angle), np.sin(angle)])
    angle = (idx[:, None] * idx[None, :] % rows) * (2.0 * math.pi / rows)
    cos, sin = np.cos(angle), np.sin(angle)
    ahead = np.block([[cos, -sin], [sin, cos]])
    back = np.block([[cos, sin], [-sin, cos]])
    last = first.T / (64 * rows)
    return (
        jnp.asarray(first, BF16),
        jnp.asarray(last, BF16),
        jnp.asarray(turn, F32),
        jnp.asarray(ahead, BF16),
        jnp.asarray(back, BF16),
    )


def mm(left, right):
    return jnp.dot(left, right, preferred_element_type=F32)


def filter_kernel(first, last, turn, slab_ref, resp_ref, *refs):
    sources, (out_ref, x_buf, h_buf, ahead, back, sems) = refs[:2], refs[2:]
    copies = fetch(sources, (ahead, back), sems)
    rows = slab_ref.shape[1]
    for ref, buf in ((slab_ref, x_buf), (resp_ref, h_buf)):
        for part in range(buf.shape[0]):
            buf[part] = ref[:, part * 128 : (part + 1) * 128].astype(F32)

    def pick_rows(buf, pick):
        return jnp.concatenate([buf[part, pick, :] for part in range(buf.shape[0])], axis=1)

    t_cos, t_sin = turn[0], turn[1]
    for copy in copies:
        copy.wait()
    group = 4
    for start in range(0, 16, group):
        picks = [pl.ds(start + at, 64, stride=16) for at in range(group)]
        turned = []
        for pick in picks:
            sect = mm(first[...], pick_rows(x_buf, pick).astype(BF16))
            re, im = sect[:64], sect[64:]
            turned.append(
                jnp.concatenate([re * t_cos + im * t_sin, im * t_cos - re * t_sin], axis=1)
            )
        spec = mm(jnp.concatenate(turned).astype(BF16), ahead[...])
        prods = []
        for at, pick in enumerate(picks):
            re, im = spec[at * 64 : (at + 1) * 64, :rows], spec[at * 64 : (at + 1) * 64, rows:]
            resp = pick_rows(h_buf, pick)
            h_re, h_im = resp[:, :rows], resp[:, rows:]
            prods.append(
                jnp.concatenate([re * h_re - im * h_im, re * h_im + im * h_re], axis=1)
            )
        inv = mm(jnp.concatenate(prods).astype(BF16), back[...])
        for at, pick in enumerate(picks):
            re, im = inv[at * 64 : (at + 1) * 64, :rows], inv[at * 64 : (at + 1) * 64, rows:]
            reverted = jnp.concatenate([re * t_cos - im * t_sin, re * t_sin + im * t_cos])
            conv = mm(last[...], reverted.astype(BF16))
            for part in range(x_buf.shape[0]):
                x_buf[part, pick, :] = conv[:, part * 128 : (part + 1) * 128]
    for part in range(x_buf.shape[0]):
        out_ref[:, part * 128 : (part + 1) * 128] = x_buf[part].astype(BF16)


def filtered(slabs, resp):
    count, rows = slabs.shape
    first, last, turn, ahead, back = tables(rows)
    return pl.pallas_call(
        filter_kernel,
        out_shape=jax.ShapeDtypeStruct((count, rows), BF16),
        in_specs=[INSIDE] * 5 + [OUTSIDE] * 2,
        out_specs=INSIDE,
        scratch_shapes=[
            pltpu.VMEM((rows // 128, count, 128), F32),
            pltpu.VMEM((2 * rows // 128, count, 128), F32),
            pltpu.VMEM((2 * rows, 2 * rows), BF16),
            pltpu.VMEM((2 * rows, 2 * rows), BF16),
            pltpu.SemaphoreType.DMA((2,)),
        ],
        compiler_params=pltpu.CompilerParams(vmem_limit_bytes=32 * 1024 * 1024),
    )(first, last, turn, *in_vmem([slabs, resp]), *in_hbm([ahead, back]))


def along_x(pieces):
    return [lax.ppermute(p, "x", shift(step)) if step else p for step, p in enumerate(pieces)]


def body(sequence_in, value_proj, gate_proj, filter_response, skip_weight, output_proj):
    rows = sequence_in.shape[0]
    half = rows // 2
    my_y, my_x, my_zl, my_c = (lax.axis_index(a) for a in ("y", "x", "zl", "c"))
    at = jnp.stack([my_y, my_x, my_c, my_zl])

    resp = turn_filter(filter_response.reshape(2 * rows, 1024))
    resp, ahead_x, ahead_c = tie(resp, my_x, my_c)
    resp = lax.all_to_all(resp.reshape(64, 16, 2 * rows), SEQ, 0, 0, tiled=True)

    wg = split_columns(ahead_x, value_proj, gate_proj)
    wg = [lax.ppermute(p, "x", shift(step)) if step else p for step, p in enumerate(wg)]
    w_x, g_x = place(my_x, wg, 2)
    my_zh = lax.axis_index("zh")

    act = lax.dynamic_slice(sequence_in, (ahead_c * half, 0), (half, sequence_in.shape[1]))
    act = lax.all_gather(act, ("x", "c"), axis=0, tiled=True)

    (w_y,) = place(my_zh, to_all(w_x, "zh"), 1)
    w_y, g_x = tie(w_y, g_x)
    w_all = to_all(w_y, "y")
    (g_y,) = place(my_zh, to_all(g_x, "zh"), 1)
    here = part_sum(at, act, [w_all[0], w_all[1], w_all[3]], (0, 1, 3))
    w_far, resp, g_y, here = tie(w_all[2], resp, g_y, here)
    g_all = lax.all_gather(g_y, "y", axis=0, tiled=True)
    *values, value = project(at, act, w_far, (2,), [here], True)
    slabs = lax.all_to_all(value, SLABS, 0, 0, tiled=True)
    values = along_x(values)
    slabs, *values = tie(slabs, *values)
    conv = filtered(slabs.reshape(1024, rows), resp.reshape(1024, 2 * rows))
    conv = conv.reshape(64, 16, rows)
    conv = lax.all_to_all(conv, SEQ, 0, 0, tiled=True).reshape(16, 4, 16, rows)
    gates = along_x(project(at, act, g_all, (0, 1, 2, 3), [], False))

    home, give = mix_and_give(
        at, conv, values, gates, skip_weight.reshape(4, 256, 1), output_proj
    )
    got = lax.ppermute(give, "c", SWAP)
    away = away_part(at, home, output_proj)
    away = (away + got.astype(F32)).astype(BF16)
    back = lax.ppermute(away, "zl", SWAP)
    home, away = tie(home, away)
    give, mine = near_parts(at, home, output_proj)
    mine = mine + lax.ppermute(give, "c", SWAP).astype(F32)
    return (mine + back.astype(F32)).astype(BF16)


def solution(mesh):
    fine = Mesh(mesh.devices.reshape(4, 4, 4, 2, 2), ("y", "zh", "x", "zl", "c"))
    tp = ("zl", "c")
    placed = (
        P(SEQ, None),
        P(SEQ, tp),
        P(SEQ, tp),
        P(None, None, SEQ, tp),
        P(tp),
        P(tp, None),
    )
    return jax.shard_map(
        body, mesh=fine, in_specs=placed, out_specs=P(SEQ, tp), check_vma=False
    )
```

```python
import math

import jax
import jax.numpy as jnp
import numpy as np
from jax import lax
from jax.experimental import pallas as pl
from jax.experimental.pallas import tpu as pltpu
from jax.sharding import Mesh
from jax.sharding import PartitionSpec as P

F32 = jnp.float32
BF16 = jnp.bfloat16
SEQ = ("y", "zh", "x")
SLABS = ("y", "zh")
SWAP = [(0, 1), (1, 0)]
INSIDE = pl.BlockSpec(memory_space=pltpu.VMEM)
OUTSIDE = pl.BlockSpec(memory_space=pltpu.HBM)
SCALARS = pl.BlockSpec(memory_space=pltpu.SMEM)


def shift(count):
    return [(i, (i + count) % 4) for i in range(4)]


def tie(*arrays):
    return lax.optimization_barrier(arrays)


def in_hbm(arrays):
    return [pltpu.with_memory_space_constraint(a, pltpu.HBM) for a in arrays]


def in_vmem(arrays):
    return [pltpu.with_memory_space_constraint(a, pltpu.VMEM) for a in arrays]


def turn_kernel(source, out):
    for part in range(4):
        block = source[:, part * 256 : (part + 1) * 256].astype(F32).T
        out[:, part] = block.astype(BF16).reshape(16, 16, block.shape[1])


def turn_filter(response):
    inside = pl.BlockSpec(memory_space=pltpu.VMEM)
    return pl.pallas_call(
        turn_kernel,
        out_shape=jax.ShapeDtypeStruct((16, 4, 16, response.shape[0]), BF16),
        in_specs=[inside],
        out_specs=inside,
    )(response)


def split_kernel(own_ref, first, second, *outs):
    rows = first.shape[0]
    for step, out in enumerate(outs):
        col = pl.multiple_of(lax.rem(own_ref[0] + step, 4) * 256, 128)
        out[:rows] = first[:, pl.ds(col, 256)]
        out[rows:] = second[:, pl.ds(col, 256)]


def split_columns(own, first, second):
    inside = pl.BlockSpec(memory_space=pltpu.VMEM)
    one = jax.ShapeDtypeStruct((2 * first.shape[0], 256), first.dtype)
    return pl.pallas_call(
        split_kernel,
        out_shape=(one,) * 4,
        in_specs=[pl.BlockSpec(memory_space=pltpu.SMEM), inside, inside],
        out_specs=(inside,) * 4,
    )(own.reshape(1), first, second)


def place_kernel(own_ref, *refs):
    sources, outs = refs[:4], refs[4:]
    rows = sources[0].shape[0] // len(outs)
    for step, source in enumerate(sources):
        row = pl.multiple_of(lax.rem(own_ref[0] + 4 - step, 4) * rows, 16)
        for at, out in enumerate(outs):
            out[pl.ds(row, rows)] = source[at * rows : (at + 1) * rows]


def place(own, pieces, count):
    inside = pl.BlockSpec(memory_space=pltpu.VMEM)
    rows, cols = pieces[0].shape
    one = jax.ShapeDtypeStruct((4 * rows // count, cols), pieces[0].dtype)
    return pl.pallas_call(
        place_kernel,
        out_shape=(one,) * count,
        in_specs=[pl.BlockSpec(memory_space=pltpu.SMEM)] + [inside] * 4,
        out_specs=(inside,) * count,
    )(own.reshape(1), *in_vmem(pieces))


def to_all(block, axis):
    return [lax.ppermute(block, axis, shift(step)) if step else block for step in range(4)]


def sum_kernel(steps, at_ref, act_ref, *refs):
    w_refs, (total, mark, a_buf, w_buf, sems) = refs[: len(steps)], refs[len(steps) :]
    depth = w_buf.shape[1]
    copies = []
    for at, step in enumerate(steps):
        first = pl.multiple_of(lax.rem(at_ref[0] + 4 - step, 4) * depth, depth)
        pair = (w_refs[at], act_ref.at[:, pl.ds(first, depth)])
        copies.append(fetch(pair, (w_buf.at[at], a_buf.at[at]), sems.at[at]))
    for at, pair in enumerate(copies):
        for copy in pair:
            copy.wait()
        prod = jnp.dot(a_buf[at], w_buf[at], preferred_element_type=F32)
        total[...] = prod if at == 0 else total[...] + prod
    mark[...] = total[:8, :128]


def part_sum(at, act, weights, steps):
    rows, depth = act.shape[0], act.shape[1] // 4
    cols = weights[0].shape[1]
    return pl.pallas_call(
        lambda *refs: sum_kernel(steps, *refs),
        out_shape=(
            jax.ShapeDtypeStruct((rows, cols), F32),
            jax.ShapeDtypeStruct((8, 128), F32),
        ),
        in_specs=[SCALARS] + [OUTSIDE] * (len(steps) + 1),
        out_specs=(INSIDE, INSIDE),
        scratch_shapes=[
            pltpu.VMEM((len(steps), rows, depth), BF16),
            pltpu.VMEM((len(steps), depth, cols), BF16),
            pltpu.SemaphoreType.DMA((len(steps), 2)),
        ],
        compiler_params=pltpu.CompilerParams(vmem_limit_bytes=40 * 1024 * 1024),
    )(at, *in_hbm([act, *weights]))


def finish_kernel(steps, whole, at_ref, act_ref, w_ref, *refs):
    a_buf, w_buf, total, sems = refs[-4:]
    outs = refs[-9:-4] if whole else refs[-8:-4]
    depth, rows = w_buf.shape[1], total.shape[0] // 4
    own_y, own_x = at_ref[0], at_ref[1]
    copies = []
    for at, step in enumerate(steps):
        first = pl.multiple_of(lax.rem(own_y + 4 - step, 4) * depth, depth)
        pair = [(act_ref.at[:, pl.ds(first, depth)], a_buf.at[at])]
        if len(steps) > 1:
            pair.append((w_ref.at[pl.ds(first, depth)], w_buf.at[at]))
        copies.append(fetch(*zip(*pair), sems.at[at]))
    for at, pair in enumerate(copies):
        for copy in pair:
            copy.wait()
        weight = w_buf[at] if len(steps) > 1 else w_ref[...]
        prod = jnp.dot(a_buf[at], weight, preferred_element_type=F32)
        if at:
            total[...] += prod
        else:
            total[...] = prod if len(steps) > 1 else refs[0][...] + prod
    for step in range(4):
        part = lax.rem(own_x + step, 4)
        row = pl.multiple_of(part * rows, 8)
        block = total[pl.ds(row, rows), :].T.astype(BF16)
        outs[step][...] = block
        if whole:
            outs[4][:, part] = block.reshape(16, 16, rows)


def project(at, act, weight, steps, before, whole):
    rows, depth = act.shape[0] // 4, act.shape[1] // 4
    cols = weight.shape[1]
    shapes = [(cols, rows)] * 4 + [(16, 4, cols // 16, rows)] * whole
    return pl.pallas_call(
        lambda *refs: finish_kernel(steps, whole, *refs),
        out_shape=[jax.ShapeDtypeStruct(shape, BF16) for shape in shapes],
        in_specs=[SCALARS, OUTSIDE] + ([INSIDE] * 3 if before else [OUTSIDE]),
        out_specs=[INSIDE] * len(shapes),
        scratch_shapes=[
            pltpu.VMEM((len(steps), 4 * rows, depth), BF16),
            pltpu.VMEM((len(steps), depth, cols), BF16),
            pltpu.VMEM((4 * rows, cols), F32),
            pltpu.SemaphoreType.DMA((len(steps), 2)),
        ],
        compiler_params=pltpu.CompilerParams(vmem_limit_bytes=40 * 1024 * 1024),
    )(at, *in_hbm([act]), *(in_vmem([weight, *before]) if before else in_hbm([weight])))


def fetch(sources, buffers, sems):
    copies = [
        pltpu.make_async_copy(src, dst, sems.at[at])
        for at, (src, dst) in enumerate(zip(sources, buffers))
    ]
    for copy in copies:
        copy.start()
    return copies


def column_block(weight_ref, block, w_buf, sem):
    col = pl.multiple_of(block * w_buf.shape[1], 128)
    return pltpu.make_async_copy(weight_ref.at[:, pl.ds(col, w_buf.shape[1])], w_buf, sem)


def mix_kernel(at_ref, skip_ref, weight_ref, conv_ref, value_ref, gate_ref, *refs):
    sources, (home_ref, give_ref, w_buf, sem, vg_buf, sems) = refs[:6], refs[6:]
    pieces = [vg_buf.at[at] for at in range(6)]
    others = fetch(sources, pieces, sems)
    values, gates = [value_ref] + pieces[:3], [gate_ref] + pieces[3:]
    own_x, own_c, own_z = at_ref[1], at_ref[2], at_ref[3]
    copy = column_block(weight_ref, 2 * (1 - own_z) + 1 - own_c, w_buf, sem)
    copy.start()
    rows = home_ref.shape[0]
    for step in range(4):
        if step == 1:
            for other in others:
                other.wait()
        src = lax.rem(own_x + 4 - step, 4)
        conv = conv_ref[:, src].astype(F32).reshape(256, rows)
        value, gate = values[step][...].astype(F32), gates[step][...].astype(F32)
        mixed = gate * (conv + skip_ref[src] * value)
        col = pl.multiple_of(src * 256, 128)
        home_ref[:, pl.ds(col, 256)] = mixed.T.astype(BF16)
    copy.wait()
    give_ref[...] = jnp.dot(home_ref[...], w_buf[...], preferred_element_type=F32).astype(BF16)


def mix_and_give(at, conv, values, gates, skip, weight):
    rows = conv.shape[-1]
    one = jax.ShapeDtypeStruct((rows, 1024), BF16)
    return pl.pallas_call(
        mix_kernel,
        out_shape=(one, one),
        in_specs=[SCALARS, INSIDE, OUTSIDE] + [INSIDE] * 3 + [OUTSIDE] * 6,
        out_specs=(INSIDE, INSIDE),
        scratch_shapes=[
            pltpu.VMEM((1024, 1024), BF16),
            pltpu.SemaphoreType.DMA,
            pltpu.VMEM((6, 256, rows), BF16),
            pltpu.SemaphoreType.DMA((6,)),
        ],
        compiler_params=pltpu.CompilerParams(vmem_limit_bytes=32 * 1024 * 1024),
    )(
        at,
        skip,
        *in_hbm([weight]),
        *in_vmem([conv, values[0], gates[0]]),
        *in_hbm([*values[1:], *gates[1:]]),
    )


def away_kernel(at_ref, home_ref, weight_ref, away_ref, w_buf, sem):
    copy = column_block(weight_ref, 2 * (1 - at_ref[3]) + at_ref[2], w_buf, sem)
    copy.start()
    copy.wait()
    away_ref[...] = jnp.dot(home_ref[...], w_buf[...], preferred_element_type=F32)


def away_part(at, home, weight):
    return pl.pallas_call(
        away_kernel,
        out_shape=jax.ShapeDtypeStruct((home.shape[0], 1024), F32),
        in_specs=[SCALARS, INSIDE, OUTSIDE],
        out_specs=INSIDE,
        scratch_shapes=[pltpu.VMEM((1024, 1024), BF16), pltpu.SemaphoreType.DMA],
        compiler_params=pltpu.CompilerParams(vmem_limit_bytes=24 * 1024 * 1024),
    )(at, home, *in_hbm([weight]))


def near_kernel(at_ref, home_ref, weight_ref, give_ref, mine_ref, w_buf, sems):
    own_z, own_c = at_ref[3], at_ref[2]
    copies = [
        column_block(weight_ref, 2 * own_z + core, w_buf.at[at], sems.at[at])
        for at, core in enumerate((1 - own_c, own_c))
    ]
    for copy in copies:
        copy.start()
    for at, out_ref in enumerate((give_ref, mine_ref)):
        copies[at].wait()
        out_ref[...] = jnp.dot(
            home_ref[...], w_buf[at], preferred_element_type=F32
        ).astype(out_ref.dtype)


def near_parts(at, home, weight):
    rows = home.shape[0]
    return pl.pallas_call(
        near_kernel,
        out_shape=(
            jax.ShapeDtypeStruct((rows, 1024), BF16),
            jax.ShapeDtypeStruct((rows, 1024), F32),
        ),
        in_specs=[SCALARS, INSIDE, OUTSIDE],
        out_specs=(INSIDE, INSIDE),
        scratch_shapes=[pltpu.VMEM((2, 1024, 1024), BF16), pltpu.SemaphoreType.DMA((2,))],
        compiler_params=pltpu.CompilerParams(vmem_limit_bytes=24 * 1024 * 1024),
    )(at, home, *in_hbm([weight]))


def tables(rows):
    slab = np.arange(64)
    angle = (slab[:, None] * slab[None, :] % 64) * (2.0 * math.pi / 64)
    first = np.concatenate([np.cos(angle), -np.sin(angle)])
    idx = np.arange(rows)
    angle = slab[:, None] * idx[None, :] * (2.0 * math.pi / (64 * rows))
    turn = np.stack([np.cos(angle), np.sin(angle)])
    angle = (idx[:, None] * idx[None, :] % rows) * (2.0 * math.pi / rows)
    cos, sin = np.cos(angle), np.sin(angle)
    ahead = np.block([[cos, -sin], [sin, cos]])
    back = np.block([[cos, sin], [-sin, cos]])
    last = first.T / (64 * rows)
    return (
        jnp.asarray(first, BF16),
        jnp.asarray(last, BF16),
        jnp.asarray(turn, F32),
        jnp.asarray(ahead, BF16),
        jnp.asarray(back, BF16),
    )


def mm(left, right):
    return jnp.dot(left, right, preferred_element_type=F32)


def filter_kernel(first, last, turn, slab_ref, resp_ref, *refs):
    sources, (out_ref, x_buf, h_buf, ahead, back, sems) = refs[:2], refs[2:]
    copies = fetch(sources, (ahead, back), sems)
    rows = slab_ref.shape[1]
    for ref, buf in ((slab_ref, x_buf), (resp_ref, h_buf)):
        for part in range(buf.shape[0]):
            buf[part] = ref[:, part * 128 : (part + 1) * 128].astype(F32)

    def pick_rows(buf, pick):
        return jnp.concatenate([buf[part, pick, :] for part in range(buf.shape[0])], axis=1)

    t_cos, t_sin = turn[0], turn[1]
    for copy in copies:
        copy.wait()
    group = 8
    for start in range(0, 16, group):
        picks = [pl.ds(start + at, 64, stride=16) for at in range(group)]
        turned = []
        for pick in picks:
            sect = mm(first[...], pick_rows(x_buf, pick).astype(BF16))
            re, im = sect[:64], sect[64:]
            turned.append(
                jnp.concatenate([re * t_cos + im * t_sin, im * t_cos - re * t_sin], axis=1)
            )
        spec = mm(jnp.concatenate(turned).astype(BF16), ahead[...])
        prods = []
        for at, pick in enumerate(picks):
            re, im = spec[at * 64 : (at + 1) * 64, :rows], spec[at * 64 : (at + 1) * 64, rows:]
            resp = pick_rows(h_buf, pick)
            h_re, h_im = resp[:, :rows], resp[:, rows:]
            prods.append(
                jnp.concatenate([re * h_re - im * h_im, re * h_im + im * h_re], axis=1)
            )
        inv = mm(jnp.concatenate(prods).astype(BF16), back[...])
        for at, pick in enumerate(picks):
            re, im = inv[at * 64 : (at + 1) * 64, :rows], inv[at * 64 : (at + 1) * 64, rows:]
            reverted = jnp.concatenate([re * t_cos - im * t_sin, re * t_sin + im * t_cos])
            conv = mm(last[...], reverted.astype(BF16))
            for part in range(x_buf.shape[0]):
                x_buf[part, pick, :] = conv[:, part * 128 : (part + 1) * 128]
    for part in range(x_buf.shape[0]):
        out_ref[:, part * 128 : (part + 1) * 128] = x_buf[part].astype(BF16)


def filtered(slabs, resp):
    count, rows = slabs.shape
    first, last, turn, ahead, back = tables(rows)
    return pl.pallas_call(
        filter_kernel,
        out_shape=jax.ShapeDtypeStruct((count, rows), BF16),
        in_specs=[INSIDE] * 5 + [OUTSIDE] * 2,
        out_specs=INSIDE,
        scratch_shapes=[
            pltpu.VMEM((rows // 128, count, 128), F32),
            pltpu.VMEM((2 * rows // 128, count, 128), F32),
            pltpu.VMEM((2 * rows, 2 * rows), BF16),
            pltpu.VMEM((2 * rows, 2 * rows), BF16),
            pltpu.SemaphoreType.DMA((2,)),
        ],
        compiler_params=pltpu.CompilerParams(vmem_limit_bytes=32 * 1024 * 1024),
    )(first, last, turn, *in_vmem([slabs, resp]), *in_hbm([ahead, back]))


def along_x(pieces):
    return [lax.ppermute(p, "x", shift(step)) if step else p for step, p in enumerate(pieces)]


def body(sequence_in, value_proj, gate_proj, filter_response, skip_weight, output_proj):
    rows = sequence_in.shape[0]
    half = rows // 2
    my_y, my_x, my_zl, my_c = (lax.axis_index(a) for a in ("y", "x", "zl", "c"))
    at = jnp.stack([my_y, my_x, my_c, my_zl])

    resp = turn_filter(filter_response.reshape(2 * rows, 1024))
    resp, ahead_x, ahead_c = tie(resp, my_x, my_c)
    resp = lax.all_to_all(resp.reshape(64, 16, 2 * rows), SEQ, 0, 0, tiled=True)

    wg = split_columns(ahead_x, value_proj, gate_proj)
    wg = [lax.ppermute(p, "x", shift(step)) if step else p for step, p in enumerate(wg)]
    w_x, g_x = place(my_x, wg, 2)
    my_zh = lax.axis_index("zh")

    act = lax.dynamic_slice(sequence_in, (ahead_c * half, 0), (half, sequence_in.shape[1]))
    act = lax.all_gather(act, ("x", "c"), axis=0, tiled=True)

    (w_y,) = place(my_zh, to_all(w_x, "zh"), 1)
    w_y, g_x = tie(w_y, g_x)
    w_all = to_all(w_y, "y")
    (g_y,) = place(my_zh, to_all(g_x, "zh"), 1)
    here, mark = part_sum(at, act, [w_all[0], w_all[1], w_all[3]], (0, 1, 3))
    w_far, resp, g_y, mark = tie(w_all[2], resp, g_y, mark)
    g_all = lax.all_gather(g_y, "y", axis=0, tiled=True)
    *values, value = project(at, act, w_far, (2,), [here, mark], True)
    slabs = lax.all_to_all(value, SLABS, 0, 0, tiled=True)
    values = along_x(values)
    slabs, *values = tie(slabs, *values)
    conv = filtered(slabs.reshape(1024, rows), resp.reshape(1024, 2 * rows))
    conv = conv.reshape(64, 16, rows)
    conv = lax.all_to_all(conv, SEQ, 0, 0, tiled=True).reshape(16, 4, 16, rows)
    gates = along_x(project(at, act, g_all, (0, 1, 2, 3), [], False))

    home, give = mix_and_give(
        at, conv, values, gates, skip_weight.reshape(4, 256, 1), output_proj
    )
    got = lax.ppermute(give, "c", SWAP)
    away = away_part(at, home, output_proj)
    away = (away + got.astype(F32)).astype(BF16)
    back = lax.ppermute(away, "zl", SWAP)
    home, away = tie(home, away)
    give, mine = near_parts(at, home, output_proj)
    mine = mine + lax.ppermute(give, "c", SWAP).astype(F32)
    return (mine + back.astype(F32)).astype(BF16)


def solution(mesh):
    fine = Mesh(mesh.devices.reshape(4, 4, 4, 2, 2), ("y", "zh", "x", "zl", "c"))
    tp = ("zl", "c")
    placed = (
        P(SEQ, None),
        P(SEQ, tp),
        P(SEQ, tp),
        P(None, None, SEQ, tp),
        P(tp),
        P(tp, None),
    )
    return jax.shard_map(
        body, mesh=fine, in_specs=placed, out_specs=P(SEQ, tp), check_vma=False
    )
```
